256 devices in a mesh: seq: 16 (over x, y), chan: 4 (over z_hi, core), dp: 4 (over z_lo).
Axes of the slice: x: 4, y: 4, z: 8 (z_hi: 2, z_lo: 4; z = z_hi * 4 + z_lo), core: 2. Of those that a mesh axis runs over, the one named last changes fastest.
Arguments:
- inputs: bfloat16 [4, 4096, 1024], P('dp', 'seq', 'chan'), may hold values from -0.046875 to 0.046875
- grad_out: bfloat16 [4, 4096, 1024], P('dp', 'seq', 'chan'), may hold values from -6 to 6
- kernel: float32 [4096, 1024], P('seq', ('chan', 'dp')), may hold values from -0.09375 to 0.09375
- skip: float32 [1024], P('chan'), may hold values from 0.5 to 1.5
Outputs:
- grad_inputs: bfloat16 [4, 4096, 1024], P('dp', 'seq', 'chan')
- grad_kernel: float32 [4096, 1024], P('seq', ('chan', 'dp'))
The draws below stay inside these ranges and needn't reach their ends.
All inputs are finite; a program needn't handle non-finite values.
Results may differ from the reference program's by a relative error of at most 0.001.
Values may be sent and summed in bfloat16 or wider, within the bound.
No kernel may reach another device: no remote copies, remote signals or barrier semaphores. Data moves between devices by JAX's collectives and lax.ppermute only.
A program may use at most 64 MiB of HBM per device.

```python
import jax
import jax.numpy as jnp
from jax import lax

C = 1024
SEQ = 4096
BATCH = 4


def steps_of(rng, extent, shards, smallest, largest):
    loudness, own = 1.0, jax.random.fold_in(rng, 6)
    for position, shards_of in shards:
        draws = jnp.exp(jax.random.uniform(jax.random.fold_in(own, position), (shards_of,), jnp.float32, smallest / len(shards), largest / len(shards)))
        loudness = loudness * jnp.repeat(draws, extent[position] // shards_of).reshape([-1 if axis == position else 1 for axis in range(len(extent))])
    return loudness


def noise(key, dims, deviation, most, shards=(), held_as=jnp.bfloat16):
    gain = steps_of(key, dims, shards, -0.22, 0.18) if shards else 1.0
    array = jax.random.normal(key, dims, jnp.float32) * deviation * gain
    return jnp.minimum(jnp.maximum(array, -most), most).astype(held_as)


def setup_inputs(seed: int = 0) -> dict:
    splits = jax.random.split(jax.random.key(seed), 5)
    return {
        "inputs": noise(splits[0], (BATCH, SEQ, C), ((SEQ * BATCH) ** -0.5), 0.046875, ((0, 4), (1, 16), (2, 4))),
        "grad_out": noise(splits[1], (BATCH, SEQ, C), 1.0, 6.0, ((0, 4), (1, 16), (2, 4))),
        "kernel": noise(splits[2], (SEQ, C), SEQ ** -0.5, 0.09375, ((0, 16), (1, 16)), jnp.float32),
        "skip": jnp.clip(0.5 + 1.0 * jax.random.uniform(splits[3], (C,), jnp.float32) ** steps_of(splits[3], (C,), ((0, 4),), -0.2, 0.2), 0.5, 1.5),
    }


def reference(inputs, grad_out, kernel, skip):
    length = 2 * SEQ
    kernel_spectrum = jnp.fft.rfft(kernel.astype(jnp.float32), n=length, axis=0)

    def per_sequence(accumulated, operands):
        signal, cotangent = operands
        cotangent_f = cotangent.astype(jnp.float32)
        signal_spectrum = jnp.fft.rfft(signal.astype(jnp.float32), n=length, axis=0)
        grad_spectrum = jnp.fft.rfft(cotangent_f, n=length, axis=0)
        correlated = jnp.fft.irfft(jnp.conj(kernel_spectrum) * grad_spectrum, n=length, axis=0)[:SEQ]
        grad_sequence = (correlated + skip[None, :] * cotangent_f).astype(jnp.bfloat16)
        return accumulated + jnp.conj(signal_spectrum) * grad_spectrum, grad_sequence

    accumulated, grad_inputs = lax.scan(per_sequence, jnp.zeros_like(kernel_spectrum), (inputs, grad_out))
    grad_kernel = jnp.fft.irfft(accumulated, n=length, axis=0)[:SEQ].astype(jnp.float32)
    return grad_inputs, grad_kernel
```

```python
import jax
import jax.numpy as jnp
from jax import lax
from jax.experimental import pallas as pl
from jax.experimental.pallas import tpu as pltpu
from jax.sharding import PartitionSpec as P

F32 = jnp.float32
BF16 = jnp.bfloat16
GROUP = ("seq", "dp")
LANES = 128
ROWS_OUT = 8
ROWS_BACK = 8


def take(stage, first, count, stride, blocks):
    return jnp.concatenate([stage[b, pl.ds(first, count, stride=stride), :] for b in blocks], axis=1)


def put(stage, first, stride, values, blocks):
    for at, b in enumerate(blocks):
        part = values[:, at * LANES : (at + 1) * LANES]
        stage[b, pl.ds(first, values.shape[0], stride=stride), :] = part


def load_all(stage, ref):
    values = ref[...].astype(F32).reshape(stage.shape[1], -1)
    for b in range(stage.shape[0]):
        stage[b] = values[:, b * LANES : (b + 1) * LANES]


def store_all(ref, stage):
    values = jnp.concatenate([stage[b] for b in range(stage.shape[0])], axis=1)
    ref[...] = values.astype(BF16).reshape(ref.shape)


def pack_kernel(u_ref, g_ref, k_ref, send_ref, stage):
    peers = send_ref.shape[0]
    piece, channels = g_ref.shape
    per_peer = channels // peers
    g_rows = g_ref[...].astype(F32).T
    u_rows = u_ref[...].astype(F32).T
    for e in range(per_peer):
        rows = slice(e * peers, (e + 1) * peers)
        put(stage, e, ROWS_OUT, g_rows[rows], (0, 1))
        put(stage, per_peer + e, ROWS_OUT, u_rows[rows], (0, 1))
    k_rows = k_ref[...].T
    high = k_rows.astype(BF16).astype(F32)
    low = k_rows - high
    for part, values in enumerate((high, low)):
        for half in range(2):
            put(stage, 2 * part + half, ROWS_OUT, values[:, half * LANES : (half + 1) * LANES], (2,))
    for row in range(4, ROWS_OUT):
        put(stage, row, ROWS_OUT, jnp.zeros((peers, LANES), F32), (2,))
    store_all(send_ref, stage)


def correlate_kernel(place_ref, skip_ref, recv_ref, back_ref, stage, shifted, hankel, toeplitz, kgrad, out):
    peers = recv_ref.shape[0]
    pieces, piece, per_peer = 16, 256, 4
    batch = peers // pieces
    place = place_ref[0]
    load_all(stage, recv_ref)
    row_ids = lax.broadcasted_iota(jnp.int32, (LANES, LANES), 0)
    col_ids = lax.broadcasted_iota(jnp.int32, (LANES, LANES), 1)
    on_or_after = col_ids >= row_ids
    after = col_ids > row_ids
    backwards = jnp.where(row_ids + col_ids == LANES - 1, 1.0, 0.0).astype(BF16)
    shifted[:, peers:, :] = jnp.zeros((2, peers, piece), F32)
    for e in range(per_peer):
        g_blocks = take(stage, e, peers, ROWS_OUT, (0, 1))
        u_blocks = take(stage, per_peer + e, peers, ROWS_OUT, (0, 1))
        shifted[0, 0:peers, :] = g_blocks
        shifted[1, 0:peers, 0:LANES] = g_blocks[:, LANES:]
        shifted[1, 0:peers, LANES:] = shifted[0, batch : peers + batch, 0:LANES]
        for step in range(pieces):
            for half in range(2):
                hankel[half * peers : (half + 1) * peers, step * piece : (step + 1) * piece] = shifted[
                    half, batch * step : batch * step + peers, :
                ].astype(BF16)
        first = per_peer * ROWS_OUT
        halves = [
            take(stage, e * ROWS_OUT + half, pieces, first, (2,))
            + take(stage, e * ROWS_OUT + 2 + half, pieces, first, (2,))
            for half in range(2)
        ]
        before = jnp.zeros((LANES, LANES), F32)
        for block in range(2 * pieces):
            values = halves[block % 2][block // 2 : block // 2 + 1, :]
            turned = pltpu.roll(jnp.broadcast_to(values, (LANES, LANES)), 0, 1, stride=1, stride_axis=0)
            square = jnp.where(on_or_after, turned, before)
            before = turned
            high = square.astype(BF16)
            columns = slice(block * LANES, (block + 1) * LANES)
            toeplitz[0:LANES, columns] = high
            toeplitz[LANES:, columns] = (square - high.astype(F32)).astype(BF16)
        both = lax.dot_general(
            hankel[...], toeplitz[...], (((1,), (1,)), ((), ())), preferred_element_type=F32
        )
        conv = both[:, 0:LANES] + both[:, LANES:]
        conv = jnp.concatenate([conv[0:peers], conv[peers:]], axis=1)
        gain = skip_ref[e * peers + place]
        put(out, e, ROWS_BACK, conv + gain * g_blocks, (0, 1))
        u_stack = jnp.concatenate([u_blocks[:, 0:LANES], u_blocks[:, LANES:]], axis=0).astype(BF16)
        u_turned = lax.dot_general(
            backwards, u_stack, (((1,), (1,)), ((), ())), preferred_element_type=F32
        ).astype(BF16)
        later = jnp.zeros((LANES, LANES), F32)
        for block in range(2 * pieces - 1, -1, -1):
            columns = slice(block * LANES, (block + 1) * LANES)
            products = jnp.dot(u_turned, hankel[:, columns], preferred_element_type=F32)
            turned = pltpu.roll(products, 1, 1, stride=1, stride_axis=0)
            lags = jnp.sum(jnp.where(after, later, turned), axis=0, keepdims=True)
            later = turned
            place_in = (block // 2) * per_peer + e
            half = block % 2
            kgrad[place_in : place_in + 1, half * LANES : (half + 1) * LANES] = lags
    lags = kgrad[...]
    high = lags.astype(BF16).astype(F32)
    put(out, per_peer, ROWS_BACK, high, (0, 1))
    put(out, per_peer + 1, ROWS_BACK, lags - high, (0, 1))
    for row in range(per_peer + 2, ROWS_BACK):
        put(out, row, ROWS_BACK, jnp.zeros((peers, piece), F32), (0, 1))
    store_all(back_ref, out)


def unpack_kernel(recv_ref, grad_inputs_ref, grad_kernel_ref, stage):
    peers = recv_ref.shape[0]
    per_peer = grad_inputs_ref.shape[1] // peers
    load_all(stage, recv_ref)
    rows = jnp.concatenate(
        [take(stage, e, peers, ROWS_BACK, (0, 1)) for e in range(per_peer)], axis=0
    )
    grad_inputs_ref[...] = rows.T.astype(BF16)
    lags = take(stage, per_peer, peers, ROWS_BACK, (0, 1)) + take(
        stage, per_peer + 1, peers, ROWS_BACK, (0, 1)
    )
    grad_kernel_ref[...] = lags.T


def shards(inputs, grad_out, kernel, skip):
    peers = lax.axis_size(GROUP)
    _, piece, channels = inputs.shape
    vmem = pl.BlockSpec(memory_space=pltpu.VMEM)
    smem = pl.BlockSpec(memory_space=pltpu.SMEM)
    params = pltpu.CompilerParams(vmem_limit_bytes=40 * 2**20)
    send = pl.pallas_call(
        pack_kernel,
        out_shape=jax.ShapeDtypeStruct((peers, ROWS_OUT, piece + LANES), BF16),
        in_specs=[vmem] * 3,
        out_specs=vmem,
        scratch_shapes=[pltpu.VMEM((3, peers * ROWS_OUT, LANES), F32)],
        compiler_params=params,
    )(inputs[0], grad_out[0], kernel)
    recv = lax.all_to_all(send, GROUP, 0, 0, tiled=True)
    place = lax.axis_index(GROUP).astype(jnp.int32).reshape(1)
    back = pl.pallas_call(
        correlate_kernel,
        out_shape=jax.ShapeDtypeStruct((peers, ROWS_BACK, piece), BF16),
        in_specs=[smem, smem, vmem],
        out_specs=vmem,
        scratch_shapes=[
            pltpu.VMEM((3, peers * ROWS_OUT, LANES), F32),
            pltpu.VMEM((2, 2 * peers, piece), F32),
            pltpu.VMEM((2 * peers, 4096), BF16),
            pltpu.VMEM((2 * LANES, 4096), BF16),
            pltpu.VMEM((peers, piece), F32),
            pltpu.VMEM((2, peers * ROWS_BACK, LANES), F32),
        ],
        compiler_params=params,
    )(place, skip, recv)
    landed = lax.all_to_all(back, GROUP, 0, 0, tiled=True)
    grad_inputs, grad_kernel = pl.pallas_call(
        unpack_kernel,
        out_shape=(
            jax.ShapeDtypeStruct((piece, channels), BF16),
            jax.ShapeDtypeStruct(kernel.shape, F32),
        ),
        in_specs=[vmem],
        out_specs=(vmem, vmem),
        scratch_shapes=[pltpu.VMEM((2, peers * ROWS_BACK, LANES), F32)],
        compiler_params=params,
    )(landed)
    return (grad_inputs[None], grad_kernel)


def solution(mesh):
    in_specs = (P("dp", "seq", "chan"), P("dp", "seq", "chan"), P("seq", ("chan", "dp")), P("chan"))
    out_specs = (P("dp", "seq", "chan"), P("seq", ("chan", "dp")))
    return jax.shard_map(shards, mesh=mesh, in_specs=in_specs, out_specs=out_specs, check_vma=False)
```

```python
import jax
import jax.numpy as jnp
from jax import lax
from jax.experimental import pallas as pl
from jax.experimental.pallas import tpu as pltpu
from jax.sharding import PartitionSpec as P

F32 = jnp.float32
BF16 = jnp.bfloat16
GROUP = ("seq", "dp")
LANES = 128
OWN = 4


def take(stage, first, count, stride, blocks):
    return jnp.concatenate([stage[b, pl.ds(first, count, stride=stride), :] for b in blocks], axis=1)


def put(stage, first, stride, values, blocks):
    for at, b in enumerate(blocks):
        part = values[:, at * LANES : (at + 1) * LANES]
        stage[b, pl.ds(first, values.shape[0], stride=stride), :] = part


def load_all(stage, ref):
    values = ref[...].astype(F32).reshape(stage.shape[1], -1)
    for b in range(stage.shape[0]):
        stage[b] = values[:, b * LANES : (b + 1) * LANES]


def store_all(ref, stage):
    values = jnp.concatenate([stage[b] for b in range(stage.shape[0])], axis=1)
    ref[...] = values.reshape(ref.shape).astype(BF16)


def pack_kernel(u_hbm, g_hbm, k_hbm, send_ref, u_ref, g_ref, k_ref, stage, sems):
    copies = [
        pltpu.make_async_copy(src, dst, sems.at[at])
        for at, (src, dst) in enumerate(((k_hbm, k_ref), (g_hbm, g_ref), (u_hbm, u_ref)))
    ]
    for copy in copies:
        copy.start()
    peers = send_ref.shape[0]
    copies[0].wait()
    k_rows = k_ref[...]
    high = k_rows.astype(BF16).astype(F32)
    low = k_rows - high
    for part, values in enumerate((high, low)):
        for half in range(2):
            put(stage, 2 * part + half, OWN, values[:, half * LANES : (half + 1) * LANES], (4,))
    for at, ref in ((1, g_ref), (2, u_ref)):
        copies[at].wait()
        rows = ref[...].astype(F32).T
        for e in range(OWN):
            put(stage, e, OWN, rows[e * peers : (e + 1) * peers], (2 * at - 2, 2 * at - 1))
    store_all(send_ref, stage)


def correlate_kernel(place_ref, skip_ref, recv_ref, back_ref, stage, shifted, hankel, toeplitz, kgrad, out):
    peers = recv_ref.shape[0]
    pieces, piece, per_peer = 16, 256, 4
    batch = peers // pieces
    place = place_ref[0]
    load_all(stage, recv_ref)
    row_ids = lax.broadcasted_iota(jnp.int32, (LANES, LANES), 0)
    col_ids = lax.broadcasted_iota(jnp.int32, (LANES, LANES), 1)
    on_or_after = col_ids >= row_ids
    after = col_ids > row_ids
    backwards = jnp.where(row_ids + col_ids == LANES - 1, 1.0, 0.0).astype(BF16)
    shifted[:, peers:, :] = jnp.zeros((2, peers, piece), F32)
    for e in range(per_peer):
        g_blocks = take(stage, e, peers, OWN, (0, 1))
        u_blocks = take(stage, e, peers, OWN, (2, 3))
        shifted[0, 0:peers, :] = g_blocks
        shifted[1, 0:peers, 0:LANES] = g_blocks[:, LANES:]
        shifted[1, 0:peers, LANES:] = shifted[0, batch : peers + batch, 0:LANES]
        for step in range(pieces):
            for half in range(2):
                hankel[half * peers : (half + 1) * peers, step * piece : (step + 1) * piece] = shifted[
                    half, batch * step : batch * step + peers, :
                ].astype(BF16)
        halves = [
            take(stage, e * OWN + half, pieces, batch * OWN, (4,))
            + take(stage, e * OWN + 2 + half, pieces, batch * OWN, (4,))
            for half in range(2)
        ]
        before = jnp.zeros((LANES, LANES), F32)
        for block in range(2 * pieces):
            values = halves[block % 2][block // 2 : block // 2 + 1, :]
            turned = pltpu.roll(jnp.broadcast_to(values, (LANES, LANES)), 0, 1, stride=1, stride_axis=0)
            square = jnp.where(on_or_after, turned, before)
            before = turned
            high = square.astype(BF16)
            columns = slice(block * LANES, (block + 1) * LANES)
            toeplitz[0:LANES, columns] = high
            toeplitz[LANES:, columns] = (square - high.astype(F32)).astype(BF16)
        both = lax.dot_general(
            hankel[...], toeplitz[...], (((1,), (1,)), ((), ())), preferred_element_type=F32
        )
        conv = both[:, 0:LANES] + both[:, LANES:]
        conv = jnp.concatenate([conv[0:peers], conv[peers:]], axis=1)
        gain = skip_ref[e * peers + place]
        put(out, e, OWN, conv + gain * g_blocks, (0, 1))
        u_stack = jnp.concatenate([u_blocks[:, 0:LANES], u_blocks[:, LANES:]], axis=0).astype(BF16)
        u_turned = lax.dot_general(
            backwards, u_stack, (((1,), (1,)), ((), ())), preferred_element_type=F32
        ).astype(BF16)
        later = jnp.zeros((LANES, LANES), F32)
        for block in range(2 * pieces - 1, -1, -1):
            columns = slice(block * LANES, (block + 1) * LANES)
            products = jnp.dot(u_turned, hankel[:, columns], preferred_element_type=F32)
            turned = pltpu.roll(products, 1, 1, stride=1, stride_axis=0)
            lags = jnp.sum(jnp.where(after, later, turned), axis=0, keepdims=True)
            later = turned
            place_in = (block // 2) * per_peer + e
            half = block % 2
            kgrad[place_in : place_in + 1, half * LANES : (half + 1) * LANES] = lags
    lags = kgrad[...]
    high = lags.astype(BF16).astype(F32)
    for part, values in enumerate((high, lags - high)):
        for half in range(2):
            put(out, 2 * part + half, OWN, values[:, half * LANES : (half + 1) * LANES], (2,))
    store_all(back_ref, out)


def unpack_kernel(recv_ref, grad_inputs_ref, grad_kernel_ref, stage):
    peers = recv_ref.shape[0]
    load_all(stage, recv_ref)
    rows = jnp.concatenate([take(stage, e, peers, OWN, (0, 1)) for e in range(OWN)], axis=0)
    grad_inputs_ref[...] = rows.T.astype(BF16)
    for half in range(2):
        grad_kernel_ref[:, half * LANES : (half + 1) * LANES] = take(
            stage, half, peers, OWN, (2,)
        ) + take(stage, 2 + half, peers, OWN, (2,))


def shards(inputs, grad_out, kernel, skip):
    peers = lax.axis_size(GROUP)
    _, piece, channels = inputs.shape
    vmem = pl.BlockSpec(memory_space=pltpu.VMEM)
    smem = pl.BlockSpec(memory_space=pltpu.SMEM)
    hbm = pl.BlockSpec(memory_space=pltpu.HBM)
    params = pltpu.CompilerParams(vmem_limit_bytes=40 * 2**20)
    fetching = pltpu.CompilerParams(vmem_limit_bytes=60 * 2**20)
    kernel_rows = kernel.T
    stage_out = pltpu.VMEM((5, peers * OWN, LANES), F32)
    stage_back = pltpu.VMEM((3, peers * OWN, LANES), F32)
    send = pl.pallas_call(
        pack_kernel,
        out_shape=jax.ShapeDtypeStruct((peers, OWN, 5 * LANES), BF16),
        in_specs=[hbm] * 3,
        out_specs=vmem,
        scratch_shapes=[
            pltpu.VMEM((piece, channels), BF16),
            pltpu.VMEM((piece, channels), BF16),
            pltpu.VMEM(kernel_rows.shape, F32),
            stage_out,
            pltpu.SemaphoreType.DMA((3,)),
        ],
        compiler_params=fetching,
    )(inputs[0], grad_out[0], kernel_rows)
    recv = lax.all_to_all(send, GROUP, 0, 0, tiled=True)
    place = lax.axis_index(GROUP).astype(jnp.int32).reshape(1)
    back = pl.pallas_call(
        correlate_kernel,
        out_shape=jax.ShapeDtypeStruct((peers, OWN, 3 * LANES), BF16),
        in_specs=[smem, smem, vmem],
        out_specs=vmem,
        scratch_shapes=[
            stage_out,
            pltpu.VMEM((2, 2 * peers, piece), F32),
            pltpu.VMEM((2 * peers, 4096), BF16),
            pltpu.VMEM((2 * LANES, 4096), BF16),
            pltpu.VMEM((peers, piece), F32),
            stage_back,
        ],
        compiler_params=params,
    )(place, skip, recv)
    landed = lax.all_to_all(back, GROUP, 0, 0, tiled=True)
    grad_inputs, grad_kernel = pl.pallas_call(
        unpack_kernel,
        out_shape=(
            jax.ShapeDtypeStruct((piece, channels), BF16),
            jax.ShapeDtypeStruct(kernel_rows.shape, F32),
        ),
        in_specs=[vmem],
        out_specs=(vmem, vmem),
        scratch_shapes=[stage_back],
        compiler_params=params,
    )(landed)
    return (grad_inputs[None], grad_kernel.T)


def solution(mesh):
    in_specs = (P("dp", "seq", "chan"), P("dp", "seq", "chan"), P("seq", ("chan", "dp")), P("chan"))
    out_specs = (P("dp", "seq", "chan"), P("seq", ("chan", "dp")))
    return jax.shard_map(shards, mesh=mesh, in_specs=in_specs, out_specs=out_specs, check_vma=False)
```

```python
import jax
import jax.numpy as jnp
from jax import lax
from jax.experimental import pallas as pl
from jax.experimental.pallas import tpu as pltpu
from jax.sharding import PartitionSpec as P

F32 = jnp.float32
BF16 = jnp.bfloat16
MESH_AXES = ("seq", "chan", "dp")
LANES = 128
OWN = 4
PIECES = 16
BATCH = 4
CHUNK = 4


def take(stage, first, count, stride, blocks):
    return jnp.concatenate([stage[b, pl.ds(first, count, stride=stride), :] for b in blocks], axis=1)


def put(stage, first, stride, values, blocks):
    for at, b in enumerate(blocks):
        part = values[:, at * LANES : (at + 1) * LANES]
        stage[b, pl.ds(first, values.shape[0], stride=stride), :] = part


def load_all(stage, ref):
    values = ref[...].astype(F32).reshape(stage.shape[1], -1)
    for b in range(stage.shape[0]):
        stage[b] = values[:, b * LANES : (b + 1) * LANES]


def store_all(ref, stage):
    values = jnp.concatenate([stage[b] for b in range(stage.shape[0])], axis=1)
    ref[...] = values.reshape(ref.shape).astype(BF16)


def pack_kernel(u_hbm, g_hbm, k_hbm, send_ref, u_ref, g_ref, k_ref, stage, sems):
    copies = [
        pltpu.make_async_copy(src, dst, sems.at[at])
        for at, (src, dst) in enumerate(((k_hbm, k_ref), (g_hbm, g_ref), (u_hbm, u_ref)))
    ]
    for copy in copies:
        copy.start()
    peers = send_ref.shape[0]
    copies[0].wait()
    k_rows = k_ref[...]
    high = k_rows.astype(BF16).astype(F32)
    low = k_rows - high
    for part, values in enumerate((high, low)):
        for half in range(2):
            put(stage, 2 * part + half, OWN, values[:, half * LANES : (half + 1) * LANES], (4,))
    for at, ref in ((1, g_ref), (2, u_ref)):
        copies[at].wait()
        rows = ref[...].astype(F32).T
        for e in range(OWN):
            put(stage, e, OWN, rows[e * peers : (e + 1) * peers], (2 * at - 2, 2 * at - 1))
    store_all(send_ref, stage)


def rows_of(b):
    return (b % 2) * 2 * PIECES + b // 2, 2


def correlate_kernel(place_ref, skip_ref, recv_ref, back_ref, stage, blocks, result, hankels, toeplitz, partial_rows, out):
    peers = recv_ref.shape[0]
    place = place_ref[0]
    piece = 2 * LANES
    load_all(stage, recv_ref)
    row_ids = lax.broadcasted_iota(jnp.int32, (LANES, LANES), 0)
    col_ids = lax.broadcasted_iota(jnp.int32, (LANES, LANES), 1)
    after = col_ids > row_ids
    backwards = jnp.where(row_ids + col_ids == LANES - 1, 1.0, 0.0).astype(BF16)
    turn = jnp.where((row_ids + col_ids) % LANES == 0, 1.0, 0.0).astype(BF16)
    stage[4] = jnp.dot(stage[4].astype(BF16), turn, preferred_element_type=F32)
    for e in range(OWN):
        for half in range(2):
            blocks[e, half, peers:, :] = jnp.zeros((peers + 8, LANES), F32)
            for kind in range(2):
                for b in range(BATCH):
                    first, step = rows_of(b)
                    values = stage[2 * kind + half, pl.ds(first * OWN + e, PIECES, stride=step * OWN), :]
                    blocks[e, 2 * kind + half, pl.ds(b, PIECES, stride=BATCH), :] = values
        k_first, k_step = rows_of(e)
        halves = [
            stage[4, pl.ds(k_first * OWN + half, PIECES, stride=k_step * OWN), :]
            + stage[4, pl.ds(k_first * OWN + 2 + half, PIECES, stride=k_step * OWN), :]
            for half in range(2)
        ]

        def later_blocks(half, lag):
            return blocks[e, half, BATCH * lag : BATCH * lag + peers, :].astype(BF16)

        def toeplitz_rows(block, before):
            values = halves[block % 2][block // 2 : block // 2 + 1, :]
            turned = pltpu.roll(jnp.broadcast_to(values, (LANES, LANES)), 0, 1, stride=1, stride_axis=0)
            square = jnp.where(col_ids <= row_ids, turned, before)
            high = square.astype(BF16)
            return jnp.concatenate([high, (square - high.astype(F32)).astype(BF16)], axis=1), turned

        def add_diagonals(block, turned, earlier):
            chosen = jnp.where(after, turned, earlier)
            partial_rows[e, 8 * block : 8 * block + 8, :] = jnp.sum(chosen.reshape(LANES // 8, 8, LANES), axis=0)

        u_stack = jnp.concatenate([blocks[e, 2, 0:peers, :], blocks[e, 3, 0:peers, :]], axis=0).astype(BF16)
        u_turned = lax.dot_general(
            backwards, u_stack, (((1,), (1,)), ((), ())), preferred_element_type=F32
        ).astype(BF16)
        before = jnp.zeros((LANES, LANES), F32)
        even = later_blocks(0, 0)
        earlier = None
        both = None
        for step in range(PIECES):
            odd, following = later_blocks(1, step), later_blocks(0, step + 1)
            hankel = jnp.concatenate(
                [jnp.concatenate([even, odd], axis=1), jnp.concatenate([odd, following], axis=1)], axis=0
            )
            even = following
            first_rows, before = toeplitz_rows(2 * step, before)
            last_rows, before = toeplitz_rows(2 * step + 1, before)
            columns = slice(step * piece, (step + 1) * piece)
            hankels[e, :, columns] = hankel
            toeplitz[e, 2 * step * LANES : (2 * step + 1) * LANES, :] = first_rows
            toeplitz[e, (2 * step + 1) * LANES : (2 * step + 2) * LANES, :] = last_rows
            if (step + 1) % CHUNK == 0:
                chunk = slice((step + 1 - CHUNK) * piece, (step + 1) * piece)
                added = jnp.dot(hankels[e, :, chunk], toeplitz[e, chunk, :], preferred_element_type=F32)
                both = added if both is None else both + added
            products = jnp.dot(u_turned, hankel, preferred_element_type=F32)
            for half in range(2):
                turned = pltpu.roll(
                    products[:, half * LANES : (half + 1) * LANES], 1, 1, stride=1, stride_axis=0
                )
                if earlier is not None:
                    add_diagonals(2 * step + half - 1, turned, earlier)
                earlier = turned
        add_diagonals(2 * PIECES - 1, jnp.zeros_like(earlier), earlier)
        for half in range(2):
            lags = sum(
                partial_rows[e, pl.ds(8 * half + row, PIECES, stride=16), :] for row in range(8)
            )
            high = lags.astype(BF16).astype(F32)
            for part, values in enumerate((high, lags - high)):
                first = k_first * OWN + 2 * part + half
                out[2, pl.ds(first, PIECES, stride=k_step * OWN), :] = values
        conv = both[:, 0:LANES] + both[:, LANES:]
        gain = skip_ref[e * peers + place]
        for half in range(2):
            result[e, half] = conv[half * peers : (half + 1) * peers] + gain * blocks[e, half, 0:peers, :]
            for b in range(BATCH):
                first, step = rows_of(b)
                out[half, pl.ds(first * OWN + e, PIECES, stride=step * OWN), :] = result[
                    e, half, pl.ds(b, PIECES, stride=BATCH), :
                ]
    store_all(back_ref, out)


def unpack_kernel(recv_ref, grad_inputs_ref, grad_kernel_ref, stage):
    peers = recv_ref.shape[0]
    load_all(stage, recv_ref)
    rows = jnp.concatenate([take(stage, e, peers, OWN, (0, 1)) for e in range(OWN)], axis=0)
    grad_inputs_ref[...] = rows.T.astype(BF16)
    for half in range(2):
        grad_kernel_ref[:, half * LANES : (half + 1) * LANES] = take(
            stage, half, peers, OWN, (2,)
        ) + take(stage, 2 + half, peers, OWN, (2,))


def exchange(blocks):
    chans = lax.axis_size("chan")
    groups = []
    for chan in range(chans):
        group = [0] * (PIECES * BATCH)
        for b in range(BATCH):
            first, step = rows_of(b)
            for piece in range(PIECES):
                group[first + step * piece] = (piece * chans + chan) * BATCH + b
        groups.append(group)
    return lax.all_to_all(blocks, MESH_AXES, 0, 0, axis_index_groups=groups, tiled=True)


def shards(inputs, grad_out, kernel, skip):
    peers = PIECES * BATCH
    _, piece, channels = inputs.shape
    vmem = pl.BlockSpec(memory_space=pltpu.VMEM)
    smem = pl.BlockSpec(memory_space=pltpu.SMEM)
    hbm = pl.BlockSpec(memory_space=pltpu.HBM)
    params = pltpu.CompilerParams(vmem_limit_bytes=40 * 2**20)
    fetching = pltpu.CompilerParams(vmem_limit_bytes=60 * 2**20)
    kernel_rows = kernel.T
    stage_out = pltpu.VMEM((5, peers * OWN, LANES), F32)
    stage_back = pltpu.VMEM((3, peers * OWN, LANES), F32)
    send = pl.pallas_call(
        pack_kernel,
        out_shape=jax.ShapeDtypeStruct((peers, OWN, 5 * LANES), BF16),
        in_specs=[hbm] * 3,
        out_specs=vmem,
        scratch_shapes=[
            pltpu.VMEM((piece, channels), BF16),
            pltpu.VMEM((piece, channels), BF16),
            pltpu.VMEM(kernel_rows.shape, F32),
            stage_out,
            pltpu.SemaphoreType.DMA((3,)),
        ],
        compiler_params=fetching,
    )(inputs[0], grad_out[0], kernel_rows)
    recv = exchange(send)
    b, piece_id = lax.axis_index("dp"), lax.axis_index("seq")
    place = ((b % 2) * 2 * PIECES + b // 2 + 2 * piece_id).astype(jnp.int32).reshape(1)
    back = pl.pallas_call(
        correlate_kernel,
        out_shape=jax.ShapeDtypeStruct((peers, OWN, 3 * LANES), BF16),
        in_specs=[smem, smem, vmem],
        out_specs=vmem,
        scratch_shapes=[
            stage_out,
            pltpu.VMEM((OWN, 4, 2 * peers + 8, LANES), F32),
            pltpu.VMEM((OWN, 2, peers, LANES), F32),
            pltpu.VMEM((OWN, 2 * peers, PIECES * piece), BF16),
            pltpu.VMEM((OWN, PIECES * piece, 2 * LANES), BF16),
            pltpu.VMEM((OWN, 16 * PIECES, LANES), F32),
            stage_back,
        ],
        compiler_params=params,
    )(place, skip, recv)
    landed = exchange(back)
    grad_inputs, grad_kernel = pl.pallas_call(
        unpack_kernel,
        out_shape=(
            jax.ShapeDtypeStruct((piece, channels), BF16),
            jax.ShapeDtypeStruct(kernel_rows.shape, F32),
        ),
        in_specs=[vmem],
        out_specs=(vmem, vmem),
        scratch_shapes=[stage_back],
        compiler_params=params,
    )(landed)
    return (grad_inputs[None], grad_kernel.T)


def solution(mesh):
    in_specs = (P("dp", "seq", "chan"), P("dp", "seq", "chan"), P("seq", ("chan", "dp")), P("chan"))
    out_specs = (P("dp", "seq", "chan"), P("seq", ("chan", "dp")))
    return jax.shard_map(shards, mesh=mesh, in_specs=in_specs, out_specs=out_specs, check_vma=False)
```

```python
import jax
import jax.numpy as jnp
from jax import lax
from jax.experimental import pallas as pl
from jax.experimental.pallas import tpu as pltpu
from jax.sharding import PartitionSpec as P

F32 = jnp.float32
BF16 = jnp.bfloat16
MESH_AXES = ("seq", "chan", "dp")
LANES = 128
OWN = 4
PIECES = 16
BATCH = 4
BLOCK = 64
CHUNK = 4


def take(stage, first, count, stride, blocks):
    return jnp.concatenate([stage[b, pl.ds(first, count, stride=stride), :] for b in blocks], axis=1)


def put(stage, first, stride, values, blocks):
    for at, b in enumerate(blocks):
        part = values[:, at * LANES : (at + 1) * LANES]
        stage[b, pl.ds(first, values.shape[0], stride=stride), :] = part


def load_all(stage, ref):
    values = ref[...].astype(F32).reshape(stage.shape[1], -1)
    for b in range(stage.shape[0]):
        stage[b] = values[:, b * LANES : (b + 1) * LANES]


def store_all(ref, stage):
    values = jnp.concatenate([stage[b] for b in range(stage.shape[0])], axis=1)
    ref[...] = values.reshape(ref.shape).astype(BF16)


def pack_kernel(u_hbm, g_hbm, k_hbm, send_ref, u_ref, g_ref, k_ref, stage, sems):
    copies = [
        pltpu.make_async_copy(src, dst, sems.at[at])
        for at, (src, dst) in enumerate(((k_hbm, k_ref), (g_hbm, g_ref), (u_hbm, u_ref)))
    ]
    for copy in copies:
        copy.start()
    peers = send_ref.shape[0]
    copies[0].wait()
    k_rows = k_ref[...]
    high = k_rows.astype(BF16).astype(F32)
    low = k_rows - high
    for part, values in enumerate((high, low)):
        for half in range(2):
            put(stage, 2 * part + half, OWN, values[:, half * LANES : (half + 1) * LANES], (4,))
    for at, ref in ((1, g_ref), (2, u_ref)):
        copies[at].wait()
        rows = ref[...].astype(F32).T
        for e in range(OWN):
            put(stage, e, OWN, rows[e * peers : (e + 1) * peers], (2 * at - 2, 2 * at - 1))
    store_all(send_ref, stage)


def rows_of(b):
    return (b % 2) * 2 * PIECES + b // 2, 2


def correlate_kernel(skip_hbm, recv_ref, back_ref, skip_ref, sem, stage, blocks, result, hankels, toeplitz, partial_rows, out):
    peers = recv_ref.shape[0]
    fetch = pltpu.make_async_copy(skip_hbm, skip_ref, sem)
    fetch.start()
    first, step = rows_of(lax.axis_index("dp"))
    place = first + step * lax.axis_index("seq")
    piece = 2 * LANES
    load_all(stage, recv_ref)
    row_ids = lax.broadcasted_iota(jnp.int32, (LANES, LANES), 0)
    col_ids = lax.broadcasted_iota(jnp.int32, (LANES, LANES), 1)
    after = col_ids[0:BLOCK] > row_ids[0:BLOCK] + BLOCK
    flip_rows = lax.broadcasted_iota(jnp.int32, (piece, piece), 0)
    flip_cols = lax.broadcasted_iota(jnp.int32, (piece, piece), 1)
    flip = jnp.where(flip_cols == flip_rows + (BLOCK - 1) - 2 * (flip_rows % BLOCK), 1.0, 0.0).astype(BF16)
    turn = jnp.where((row_ids + col_ids) % LANES == 0, 1.0, 0.0).astype(BF16)
    stage[4] = jnp.dot(stage[4].astype(BF16), turn, preferred_element_type=F32)
    for e in range(OWN):
        for half in range(2):
            blocks[e, half, peers:, :] = jnp.zeros((peers + 8, LANES), F32)
            for kind in range(2):
                for b in range(BATCH):
                    first, step = rows_of(b)
                    values = stage[2 * kind + half, pl.ds(first * OWN + e, PIECES, stride=step * OWN), :]
                    blocks[e, 2 * kind + half, pl.ds(b, PIECES, stride=BATCH), :] = values
        k_first, k_step = rows_of(e)
        halves = [
            stage[4, pl.ds(k_first * OWN + half, PIECES, stride=k_step * OWN), :]
            + stage[4, pl.ds(k_first * OWN + 2 + half, PIECES, stride=k_step * OWN), :]
            for half in range(2)
        ]

        def later_blocks(half, lag):
            return blocks[e, half, BATCH * lag : BATCH * lag + peers, :].astype(BF16)

        def toeplitz_rows(block, before):
            values = halves[block % 2][block // 2 : block // 2 + 1, :]
            turned = pltpu.roll(jnp.broadcast_to(values, (LANES, LANES)), 0, 1, stride=1, stride_axis=0)
            square = jnp.where(col_ids <= row_ids, turned, before)
            high = square.astype(BF16)
            return jnp.concatenate([high, (square - high.astype(F32)).astype(BF16)], axis=1), turned

        def add_diagonals(block, turned, earlier):
            chosen = jnp.where(after, turned, earlier)
            partial_rows[e, 8 * block : 8 * block + 8, :] = jnp.sum(chosen.reshape(BLOCK // 8, 8, LANES), axis=0)

        left, right = blocks[e, 0, 0:peers, :], blocks[e, 1, 0:peers, :]
        following = blocks[e, 0, BATCH : peers + BATCH, :]
        blocks[e, 4, 0:peers, :] = jnp.concatenate([left[:, BLOCK:], right[:, :BLOCK]], axis=1)
        blocks[e, 5, 0:peers, :] = jnp.concatenate([right[:, BLOCK:], following[:, :BLOCK]], axis=1)
        for half in range(2):
            blocks[e, 4 + half, peers:, :] = jnp.zeros((peers + 8, LANES), F32)
        u_rows = jnp.concatenate([blocks[e, 2, 0:peers, :], blocks[e, 3, 0:peers, :]], axis=1).astype(BF16)
        u_turned = lax.dot_general(flip, u_rows, (((1,), (1,)), ((), ())), preferred_element_type=F32)
        u_turned = jnp.concatenate(
            [u_turned[at * BLOCK : (at + 1) * BLOCK] for at in (0, 2, 1, 3)], axis=1
        ).astype(BF16)
        before = jnp.zeros((LANES, LANES), F32)
        now = [later_blocks(at, 0) for at in (0, 4)]
        earlier = None
        both = None
        for step in range(PIECES):
            odd = [later_blocks(at, step) for at in (1, 5)]
            following = [later_blocks(at, step + 1) for at in (0, 4)]
            hankel = jnp.concatenate(
                [
                    jnp.concatenate(pair, axis=1)
                    for at in range(2)
                    for pair in ((now[at], odd[at]), (odd[at], following[at]))
                ],
                axis=0,
            )
            now = following
            first_rows, before = toeplitz_rows(2 * step, before)
            last_rows, before = toeplitz_rows(2 * step + 1, before)
            columns = slice(step * piece, (step + 1) * piece)
            hankels[e, :, columns] = hankel[0 : 2 * peers]
            toeplitz[e, 2 * step * LANES : (2 * step + 1) * LANES, :] = first_rows
            toeplitz[e, (2 * step + 1) * LANES : (2 * step + 2) * LANES, :] = last_rows
            if (step + 1) % CHUNK == 0:
                chunk = slice((step + 1 - CHUNK) * piece, (step + 1) * piece)
                added = jnp.dot(hankels[e, :, chunk], toeplitz[e, chunk, :], preferred_element_type=F32)
                both = added if both is None else both + added
            products = jnp.dot(u_turned, hankel, preferred_element_type=F32)
            for half in range(2):
                turned = pltpu.roll(
                    products[:, half * LANES : (half + 1) * LANES], BLOCK + 1, 1, stride=1, stride_axis=0
                )
                if earlier is not None:
                    add_diagonals(2 * step + half - 1, turned, earlier)
                earlier = turned
        add_diagonals(2 * PIECES - 1, jnp.zeros_like(earlier), earlier)
        for half in range(2):
            lags = sum(
                partial_rows[e, pl.ds(8 * half + row, PIECES, stride=16), :] for row in range(8)
            )
            high = lags.astype(BF16).astype(F32)
            for part, values in enumerate((high, lags - high)):
                first = k_first * OWN + 2 * part + half
                out[2, pl.ds(first, PIECES, stride=k_step * OWN), :] = values
        conv = both[:, 0:LANES] + both[:, LANES:]
        if e == 0:
            fetch.wait()
        gain = skip_ref[e * peers + place]
        for half in range(2):
            result[e, half] = conv[half * peers : (half + 1) * peers] + gain * blocks[e, half, 0:peers, :]
            for b in range(BATCH):
                first, step = rows_of(b)
                out[half, pl.ds(first * OWN + e, PIECES, stride=step * OWN), :] = result[
                    e, half, pl.ds(b, PIECES, stride=BATCH), :
                ]
    store_all(back_ref, out)


def unpack_kernel(recv_ref, grad_inputs_ref, grad_kernel_ref, stage):
    peers = recv_ref.shape[0]
    load_all(stage, recv_ref)
    rows = jnp.concatenate([take(stage, e, peers, OWN, (0, 1)) for e in range(OWN)], axis=0)
    grad_inputs_ref[...] = rows.T.astype(BF16)
    for half in range(2):
        grad_kernel_ref[:, half * LANES : (half + 1) * LANES] = take(
            stage, half, peers, OWN, (2,)
        ) + take(stage, 2 + half, peers, OWN, (2,))


def exchange(blocks):
    chans = lax.axis_size("chan")
    groups = []
    for chan in range(chans):
        group = [0] * (PIECES * BATCH)
        for b in range(BATCH):
            first, step = rows_of(b)
            for piece in range(PIECES):
                group[first + step * piece] = (piece * chans + chan) * BATCH + b
        groups.append(group)
    return lax.all_to_all(blocks, MESH_AXES, 0, 0, axis_index_groups=groups, tiled=True)


def shards(inputs, grad_out, kernel, skip):
    peers = PIECES * BATCH
    _, piece, channels = inputs.shape
    vmem = pl.BlockSpec(memory_space=pltpu.VMEM)
    hbm = pl.BlockSpec(memory_space=pltpu.HBM)
    params = pltpu.CompilerParams(vmem_limit_bytes=40 * 2**20)
    fetching = pltpu.CompilerParams(vmem_limit_bytes=60 * 2**20)
    kernel_rows = kernel.T
    stage_out = pltpu.VMEM((5, peers * OWN, LANES), F32)
    stage_back = pltpu.VMEM((3, peers * OWN, LANES), F32)
    send = pl.pallas_call(
        pack_kernel,
        out_shape=jax.ShapeDtypeStruct((peers, OWN, 5 * LANES), BF16),
        in_specs=[hbm] * 3,
        out_specs=vmem,
        scratch_shapes=[
            pltpu.VMEM((piece, channels), BF16),
            pltpu.VMEM((piece, channels), BF16),
            pltpu.VMEM(kernel_rows.shape, F32),
            stage_out,
            pltpu.SemaphoreType.DMA((3,)),
        ],
        compiler_params=fetching,
    )(inputs[0], grad_out[0], kernel_rows)
    recv = exchange(send)
    back = pl.pallas_call(
        correlate_kernel,
        out_shape=jax.ShapeDtypeStruct((peers, OWN, 3 * LANES), BF16),
        in_specs=[hbm, vmem],
        out_specs=vmem,
        scratch_shapes=[
            pltpu.SMEM(skip.shape, F32),
            pltpu.SemaphoreType.DMA(()),
            stage_out,
            pltpu.VMEM((OWN, 6, 2 * peers + 8, LANES), F32),
            pltpu.VMEM((OWN, 2, peers, LANES), F32),
            pltpu.VMEM((OWN, 2 * peers, PIECES * piece), BF16),
            pltpu.VMEM((OWN, PIECES * piece, 2 * LANES), BF16),
            pltpu.VMEM((OWN, 16 * PIECES, LANES), F32),
            stage_back,
        ],
        compiler_params=params,
    )(skip, recv)
    landed = exchange(back)
    grad_inputs, grad_kernel = pl.pallas_call(
        unpack_kernel,
        out_shape=(
            jax.ShapeDtypeStruct((piece, channels), BF16),
            jax.ShapeDtypeStruct(kernel_rows.shape, F32),
        ),
        in_specs=[vmem],
        out_specs=(vmem, vmem),
        scratch_shapes=[stage_back],
        compiler_params=params,
    )(landed)
    return (grad_inputs[None], grad_kernel.T)


def solution(mesh):
    in_specs = (P("dp", "seq", "chan"), P("dp", "seq", "chan"), P("seq", ("chan", "dp")), P("chan"))
    out_specs = (P("dp", "seq", "chan"), P("seq", ("chan", "dp")))
    return jax.shard_map(shards, mesh=mesh, in_specs=in_specs, out_specs=out_specs, check_vma=False)
```

```python
import jax
import jax.numpy as jnp
from jax import lax
from jax.experimental import pallas as pl
from jax.experimental.pallas import tpu as pltpu
from jax.sharding import PartitionSpec as P

F32 = jnp.float32
BF16 = jnp.bfloat16
MESH_AXES = ("seq", "chan", "dp")
LANES = 128
OWN = 4
PIECES = 16
BATCH = 4
BLOCK = 64


def take(stage, first, count, stride, blocks):
    return jnp.concatenate([stage[b, pl.ds(first, count, stride=stride), :] for b in blocks], axis=1)


def put(stage, first, stride, values, blocks):
    for at, b in enumerate(blocks):
        part = values[:, at * LANES : (at + 1) * LANES]
        stage[b, pl.ds(first, values.shape[0], stride=stride), :] = part


def load_all(stage, ref):
    values = ref[...].astype(F32).reshape(stage.shape[1], -1)
    for b in range(stage.shape[0]):
        stage[b] = values[:, b * LANES : (b + 1) * LANES]


def store_all(ref, stage):
    values = jnp.concatenate([stage[b] for b in range(stage.shape[0])], axis=1)
    ref[...] = values.reshape(ref.shape).astype(BF16)


def pack_kernel(u_hbm, g_hbm, k_hbm, send_ref, u_ref, g_ref, k_ref, stage, sems):
    copies = [
        pltpu.make_async_copy(src, dst, sems.at[at])
        for at, (src, dst) in enumerate(((k_hbm, k_ref), (g_hbm, g_ref), (u_hbm, u_ref)))
    ]
    for copy in copies:
        copy.start()
    peers = send_ref.shape[0]
    copies[0].wait()
    k_rows = k_ref[...]
    high = k_rows.astype(BF16).astype(F32)
    low = k_rows - high
    for part, values in enumerate((high, low)):
        for half in range(2):
            put(stage, 2 * part + half, OWN, values[:, half * LANES : (half + 1) * LANES], (4,))
    for at, ref in ((1, g_ref), (2, u_ref)):
        copies[at].wait()
        rows = ref[...].astype(F32).T
        for e in range(OWN):
            put(stage, e, OWN, rows[e * peers : (e + 1) * peers], (2 * at - 2, 2 * at - 1))
    store_all(send_ref, stage)


def rows_of(b):
    return (b % 2) * 2 * PIECES + b // 2, 2


def correlate_kernel(skip_hbm, recv_ref, back_ref, skip_ref, sem, stage, blocks, result, partial_rows, out):
    peers = recv_ref.shape[0]
    fetch = pltpu.make_async_copy(skip_hbm, skip_ref, sem)
    fetch.start()
    first, step = rows_of(lax.axis_index("dp"))
    place = first + step * lax.axis_index("seq")
    piece = 2 * LANES
    load_all(stage, recv_ref)
    row_ids = lax.broadcasted_iota(jnp.int32, (LANES, LANES), 0)
    col_ids = lax.broadcasted_iota(jnp.int32, (LANES, LANES), 1)
    after = col_ids[0:BLOCK] > row_ids[0:BLOCK] + BLOCK
    flip_rows = lax.broadcasted_iota(jnp.int32, (piece, piece), 0)
    flip_cols = lax.broadcasted_iota(jnp.int32, (piece, piece), 1)
    flip = jnp.where(flip_cols == flip_rows + (BLOCK - 1) - 2 * (flip_rows % BLOCK), 1.0, 0.0).astype(BF16)
    turn = jnp.where((row_ids + col_ids) % LANES == 0, 1.0, 0.0).astype(BF16)
    stage[4] = jnp.dot(stage[4].astype(BF16), turn, preferred_element_type=F32)
    for e in range(OWN):
        for half in range(2):
            blocks[e, half, peers:, :] = jnp.zeros((peers + 8, LANES), F32)
            for kind in range(2):
                for b in range(BATCH):
                    first, step = rows_of(b)
                    values = stage[2 * kind + half, pl.ds(first * OWN + e, PIECES, stride=step * OWN), :]
                    blocks[e, 2 * kind + half, pl.ds(b, PIECES, stride=BATCH), :] = values
        k_first, k_step = rows_of(e)
        halves = [
            stage[4, pl.ds(k_first * OWN + half, PIECES, stride=k_step * OWN), :]
            + stage[4, pl.ds(k_first * OWN + 2 + half, PIECES, stride=k_step * OWN), :]
            for half in range(2)
        ]

        def later_blocks(half, lag):
            return blocks[e, half, BATCH * lag : BATCH * lag + peers, :].astype(BF16)

        def toeplitz_rows(block, before):
            values = halves[block % 2][block // 2 : block // 2 + 1, :]
            turned = pltpu.roll(jnp.broadcast_to(values, (LANES, LANES)), 0, 1, stride=1, stride_axis=0)
            square = jnp.where(col_ids <= row_ids, turned, before)
            high = square.astype(BF16)
            return jnp.concatenate([high, (square - high.astype(F32)).astype(BF16)], axis=1), turned

        def add_diagonals(block, turned, earlier):
            chosen = jnp.where(after, turned, earlier)
            partial_rows[e, 8 * block : 8 * block + 8, :] = jnp.sum(chosen.reshape(BLOCK // 8, 8, LANES), axis=0)

        left, right = blocks[e, 0, 0:peers, :], blocks[e, 1, 0:peers, :]
        following = blocks[e, 0, BATCH : peers + BATCH, :]
        blocks[e, 4, 0:peers, :] = jnp.concatenate([left[:, BLOCK:], right[:, :BLOCK]], axis=1)
        blocks[e, 5, 0:peers, :] = jnp.concatenate([right[:, BLOCK:], following[:, :BLOCK]], axis=1)
        for half in range(2):
            blocks[e, 4 + half, peers:, :] = jnp.zeros((peers + 8, LANES), F32)
        u_rows = jnp.concatenate([blocks[e, 2, 0:peers, :], blocks[e, 3, 0:peers, :]], axis=1).astype(BF16)
        u_turned = lax.dot_general(flip, u_rows, (((1,), (1,)), ((), ())), preferred_element_type=F32)
        u_turned = jnp.concatenate(
            [u_turned[at * BLOCK : (at + 1) * BLOCK] for at in (0, 2, 1, 3)], axis=1
        ).astype(BF16)
        before = jnp.zeros((LANES, LANES), F32)
        now = [later_blocks(at, 0) for at in (0, 4)]
        earlier = None
        both = None
        for step in range(PIECES):
            odd = [later_blocks(at, step) for at in (1, 5)]
            following = [later_blocks(at, step + 1) for at in (0, 4)]
            hankel = jnp.concatenate(
                [
                    jnp.concatenate(pair, axis=1)
                    for at in range(2)
                    for pair in ((now[at], odd[at]), (odd[at], following[at]))
                ],
                axis=0,
            )
            now = following
            first_rows, before = toeplitz_rows(2 * step, before)
            last_rows, before = toeplitz_rows(2 * step + 1, before)
            added = jnp.dot(
                hankel[0 : 2 * peers],
                jnp.concatenate([first_rows, last_rows], axis=0),
                preferred_element_type=F32,
            )
            both = added if both is None else both + added
            products = jnp.dot(u_turned, hankel, preferred_element_type=F32)
            for half in range(2):
                turned = pltpu.roll(
                    products[:, half * LANES : (half + 1) * LANES], BLOCK + 1, 1, stride=1, stride_axis=0
                )
                if earlier is not None:
                    add_diagonals(2 * step + half - 1, turned, earlier)
                earlier = turned
        add_diagonals(2 * PIECES - 1, jnp.zeros_like(earlier), earlier)
        for half in range(2):
            lags = sum(
                partial_rows[e, pl.ds(8 * half + row, PIECES, stride=16), :] for row in range(8)
            )
            high = lags.astype(BF16).astype(F32)
            for part, values in enumerate((high, lags - high)):
                first = k_first * OWN + 2 * part + half
                out[2, pl.ds(first, PIECES, stride=k_step * OWN), :] = values
        conv = both[:, 0:LANES] + both[:, LANES:]
        if e == 0:
            fetch.wait()
        gain = skip_ref[e * peers + place]
        for half in range(2):
            result[e, half] = conv[half * peers : (half + 1) * peers] + gain * blocks[e, half, 0:peers, :]
            for b in range(BATCH):
                first, step = rows_of(b)
                out[half, pl.ds(first * OWN + e, PIECES, stride=step * OWN), :] = result[
                    e, half, pl.ds(b, PIECES, stride=BATCH), :
                ]
    store_all(back_ref, out)


def unpack_kernel(recv_ref, grad_inputs_ref, grad_kernel_ref, stage):
    peers = recv_ref.shape[0]
    load_all(stage, recv_ref)
    rows = jnp.concatenate([take(stage, e, peers, OWN, (0, 1)) for e in range(OWN)], axis=0)
    grad_inputs_ref[...] = rows.T.astype(BF16)
    for half in range(2):
        grad_kernel_ref[:, half * LANES : (half + 1) * LANES] = take(
            stage, half, peers, OWN, (2,)
        ) + take(stage, 2 + half, peers, OWN, (2,))


def exchange(blocks):
    chans = lax.axis_size("chan")
    groups = []
    for chan in range(chans):
        group = [0] * (PIECES * BATCH)
        for b in range(BATCH):
            first, step = rows_of(b)
            for piece in range(PIECES):
                group[first + step * piece] = (piece * chans + chan) * BATCH + b
        groups.append(group)
    return lax.all_to_all(blocks, MESH_AXES, 0, 0, axis_index_groups=groups, tiled=True)


def shards(inputs, grad_out, kernel, skip):
    peers = PIECES * BATCH
    _, piece, channels = inputs.shape
    vmem = pl.BlockSpec(memory_space=pltpu.VMEM)
    hbm = pl.BlockSpec(memory_space=pltpu.HBM)
    params = pltpu.CompilerParams(vmem_limit_bytes=40 * 2**20)
    fetching = pltpu.CompilerParams(vmem_limit_bytes=60 * 2**20)
    kernel_rows = kernel.T
    stage_out = pltpu.VMEM((5, peers * OWN, LANES), F32)
    stage_back = pltpu.VMEM((3, peers * OWN, LANES), F32)
    send = pl.pallas_call(
        pack_kernel,
        out_shape=jax.ShapeDtypeStruct((peers, OWN, 5 * LANES), BF16),
        in_specs=[hbm] * 3,
        out_specs=vmem,
        scratch_shapes=[
            pltpu.VMEM((piece, channels), BF16),
            pltpu.VMEM((piece, channels), BF16),
            pltpu.VMEM(kernel_rows.shape, F32),
            stage_out,
            pltpu.SemaphoreType.DMA((3,)),
        ],
        compiler_params=fetching,
    )(inputs[0], grad_out[0], kernel_rows)
    recv = exchange(send)
    back = pl.pallas_call(
        correlate_kernel,
        out_shape=jax.ShapeDtypeStruct((peers, OWN, 3 * LANES), BF16),
        in_specs=[hbm, vmem],
        out_specs=vmem,
        scratch_shapes=[
            pltpu.SMEM(skip.shape, F32),
            pltpu.SemaphoreType.DMA(()),
            stage_out,
            pltpu.VMEM((OWN, 6, 2 * peers + 8, LANES), F32),
            pltpu.VMEM((OWN, 2, peers, LANES), F32),
            pltpu.VMEM((OWN, 16 * PIECES, LANES), F32),
            stage_back,
        ],
        compiler_params=params,
    )(skip, recv)
    landed = exchange(back)
    grad_inputs, grad_kernel = pl.pallas_call(
        unpack_kernel,
        out_shape=(
            jax.ShapeDtypeStruct((piece, channels), BF16),
            jax.ShapeDtypeStruct(kernel_rows.shape, F32),
        ),
        in_specs=[vmem],
        out_specs=(vmem, vmem),
        scratch_shapes=[stage_back],
        compiler_params=params,
    )(landed)
    return (grad_inputs[None], grad_kernel.T)


def solution(mesh):
    in_specs = (P("dp", "seq", "chan"), P("dp", "seq", "chan"), P("seq", ("chan", "dp")), P("chan"))
    out_specs = (P("dp", "seq", "chan"), P("seq", ("chan", "dp")))
    return jax.shard_map(shards, mesh=mesh, in_specs=in_specs, out_specs=out_specs, check_vma=False)
```

```python
import jax
import jax.numpy as jnp
from jax import lax
from jax.experimental import pallas as pl
from jax.experimental.pallas import tpu as pltpu
from jax.sharding import PartitionSpec as P

F32 = jnp.float32
BF16 = jnp.bfloat16
MESH_AXES = ("seq", "chan", "dp")
LANES = 128
OWN = 4
PIECES = 16
BATCH = 4
BLOCK = 64


def take(stage, first, count, stride, blocks):
    return jnp.concatenate([stage[b, pl.ds(first, count, stride=stride), :] for b in blocks], axis=1)


def put(stage, first, stride, values, blocks):
    for at, b in enumerate(blocks):
        part = values[:, at * LANES : (at + 1) * LANES]
        stage[b, pl.ds(first, values.shape[0], stride=stride), :] = part


def load_all(stage, ref):
    values = ref[...].astype(F32).reshape(stage.shape[1], -1)
    for b in range(stage.shape[0]):
        stage[b] = values[:, b * LANES : (b + 1) * LANES]


def store_all(ref, stage):
    values = jnp.concatenate([stage[b] for b in range(stage.shape[0])], axis=1)
    ref[...] = values.reshape(ref.shape).astype(BF16)


def pack_kernel(u_hbm, g_hbm, k_hbm, send_ref, u_ref, g_ref, k_ref, stage, sems):
    copies = [
        pltpu.make_async_copy(src, dst, sems.at[at])
        for at, (src, dst) in enumerate(((k_hbm, k_ref), (g_hbm, g_ref), (u_hbm, u_ref)))
    ]
    for copy in copies:
        copy.start()
    peers = send_ref.shape[0]
    copies[0].wait()
    k_rows = k_ref[...]
    high = k_rows.astype(BF16).astype(F32)
    low = k_rows - high
    for part, values in enumerate((high, low)):
        for half in range(2):
            put(stage, 2 * part + half, OWN, values[:, half * LANES : (half + 1) * LANES], (4,))
    for at, ref in ((1, g_ref), (2, u_ref)):
        copies[at].wait()
        rows = ref[...].astype(F32).T
        for e in range(OWN):
            put(stage, e, OWN, rows[e * peers : (e + 1) * peers], (2 * at - 2, 2 * at - 1))
    store_all(send_ref, stage)


def rows_of(b):
    return (b % 2) * 2 * PIECES + 1 - b // 2, 2


def correlate_kernel(skip_hbm, recv_ref, back_ref, skip_ref, sem, stage, blocks, result, partial_rows, out):
    peers = recv_ref.shape[0]
    fetch = pltpu.make_async_copy(skip_hbm, skip_ref, sem)
    fetch.start()
    first, step = rows_of(lax.axis_index("dp"))
    place = first + step * lax.axis_index("seq")
    piece = 2 * LANES
    load_all(stage, recv_ref)
    row_ids = lax.broadcasted_iota(jnp.int32, (LANES, LANES), 0)
    col_ids = lax.broadcasted_iota(jnp.int32, (LANES, LANES), 1)
    after = col_ids[0:BLOCK] > row_ids[0:BLOCK] + BLOCK
    flip_rows = lax.broadcasted_iota(jnp.int32, (piece, piece), 0)
    flip_cols = lax.broadcasted_iota(jnp.int32, (piece, piece), 1)
    flip = jnp.where(flip_cols == flip_rows + (BLOCK - 1) - 2 * (flip_rows % BLOCK), 1.0, 0.0).astype(BF16)
    turn = jnp.where((row_ids + col_ids) % LANES == 0, 1.0, 0.0).astype(BF16)
    stage[4] = jnp.dot(stage[4].astype(BF16), turn, preferred_element_type=F32)
    for e in range(OWN):
        for half in range(2):
            blocks[e, half, peers:, :] = jnp.zeros((peers + 8, LANES), F32)
            for kind in range(2):
                for b in range(BATCH):
                    first, step = rows_of(b)
                    values = stage[2 * kind + half, pl.ds(first * OWN + e, PIECES, stride=step * OWN), :]
                    blocks[e, 2 * kind + half, pl.ds(b, PIECES, stride=BATCH), :] = values
        k_first, k_step = rows_of(e)
        halves = [
            stage[4, pl.ds(k_first * OWN + half, PIECES, stride=k_step * OWN), :]
            + stage[4, pl.ds(k_first * OWN + 2 + half, PIECES, stride=k_step * OWN), :]
            for half in range(2)
        ]

        def later_blocks(half, lag):
            return blocks[e, half, BATCH * lag : BATCH * lag + peers, :].astype(BF16)

        def toeplitz_rows(block, before):
            values = halves[block % 2][block // 2 : block // 2 + 1, :]
            turned = pltpu.roll(jnp.broadcast_to(values, (LANES, LANES)), 0, 1, stride=1, stride_axis=0)
            square = jnp.where(col_ids <= row_ids, turned, before)
            high = square.astype(BF16)
            return jnp.concatenate([high, (square - high.astype(F32)).astype(BF16)], axis=1), turned

        def add_diagonals(block, turned, earlier):
            chosen = jnp.where(after, turned, earlier)
            partial_rows[e, 8 * block : 8 * block + 8, :] = jnp.sum(chosen.reshape(BLOCK // 8, 8, LANES), axis=0)

        left, right = blocks[e, 0, 0:peers, :], blocks[e, 1, 0:peers, :]
        following = blocks[e, 0, BATCH : peers + BATCH, :]
        blocks[e, 4, 0:peers, :] = jnp.concatenate([left[:, BLOCK:], right[:, :BLOCK]], axis=1)
        blocks[e, 5, 0:peers, :] = jnp.concatenate([right[:, BLOCK:], following[:, :BLOCK]], axis=1)
        for half in range(2):
            blocks[e, 4 + half, peers:, :] = jnp.zeros((peers + 8, LANES), F32)
        u_rows = jnp.concatenate([blocks[e, 2, 0:peers, :], blocks[e, 3, 0:peers, :]], axis=1).astype(BF16)
        u_turned = lax.dot_general(flip, u_rows, (((1,), (1,)), ((), ())), preferred_element_type=F32)
        u_turned = jnp.concatenate(
            [u_turned[at * BLOCK : (at + 1) * BLOCK] for at in (0, 2, 1, 3)], axis=1
        ).astype(BF16)
        before = jnp.zeros((LANES, LANES), F32)
        now = [later_blocks(at, 0) for at in (0, 4)]
        earlier = None
        both = None
        for step in range(PIECES):
            odd = [later_blocks(at, step) for at in (1, 5)]
            following = [later_blocks(at, step + 1) for at in (0, 4)]
            hankel = jnp.concatenate(
                [
                    jnp.concatenate(pair, axis=1)
                    for at in range(2)
                    for pair in ((now[at], odd[at]), (odd[at], following[at]))
                ],
                axis=0,
            )
            now = following
            first_rows, before = toeplitz_rows(2 * step, before)
            last_rows, before = toeplitz_rows(2 * step + 1, before)
            added = jnp.dot(
                hankel[0 : 2 * peers],
                jnp.concatenate([first_rows, last_rows], axis=0),
                preferred_element_type=F32,
            )
            both = added if both is None else both + added
            products = jnp.dot(u_turned, hankel, preferred_element_type=F32)
            for half in range(2):
                turned = pltpu.roll(
                    products[:, half * LANES : (half + 1) * LANES], BLOCK + 1, 1, stride=1, stride_axis=0
                )
                if earlier is not None:
                    add_diagonals(2 * step + half - 1, turned, earlier)
                earlier = turned
        add_diagonals(2 * PIECES - 1, jnp.zeros_like(earlier), earlier)
        for half in range(2):
            lags = sum(
                partial_rows[e, pl.ds(8 * half + row, PIECES, stride=16), :] for row in range(8)
            )
            high = lags.astype(BF16).astype(F32)
            for part, values in enumerate((high, lags - high)):
                first = k_first * OWN + 2 * part + half
                out[2, pl.ds(first, PIECES, stride=k_step * OWN), :] = values
        conv = both[:, 0:LANES] + both[:, LANES:]
        if e == 0:
            fetch.wait()
        gain = skip_ref[e * peers + place]
        for half in range(2):
            result[e, half] = conv[half * peers : (half + 1) * peers] + gain * blocks[e, half, 0:peers, :]
            for b in range(BATCH):
                first, step = rows_of(b)
                out[half, pl.ds(first * OWN + e, PIECES, stride=step * OWN), :] = result[
                    e, half, pl.ds(b, PIECES, stride=BATCH), :
                ]
    store_all(back_ref, out)


def unpack_kernel(recv_ref, grad_inputs_ref, grad_kernel_ref, stage):
    peers = recv_ref.shape[0]
    load_all(stage, recv_ref)
    rows = jnp.concatenate([take(stage, e, peers, OWN, (0, 1)) for e in range(OWN)], axis=0)
    grad_inputs_ref[...] = rows.T.astype(BF16)
    for half in range(2):
        grad_kernel_ref[:, half * LANES : (half + 1) * LANES] = take(
            stage, half, peers, OWN, (2,)
        ) + take(stage, 2 + half, peers, OWN, (2,))


def exchange(blocks):
    chans = lax.axis_size("chan")
    groups = []
    for chan in range(chans):
        group = [0] * (PIECES * BATCH)
        for b in range(BATCH):
            first, step = rows_of(b)
            for piece in range(PIECES):
                group[first + step * piece] = (piece * chans + chan) * BATCH + b
        groups.append(group)
    return lax.all_to_all(blocks, MESH_AXES, 0, 0, axis_index_groups=groups, tiled=True)


def shards(inputs, grad_out, kernel, skip):
    peers = PIECES * BATCH
    _, piece, channels = inputs.shape
    vmem = pl.BlockSpec(memory_space=pltpu.VMEM)
    hbm = pl.BlockSpec(memory_space=pltpu.HBM)
    params = pltpu.CompilerParams(vmem_limit_bytes=40 * 2**20)
    fetching = pltpu.CompilerParams(vmem_limit_bytes=60 * 2**20)
    kernel_rows = kernel.T
    stage_out = pltpu.VMEM((5, peers * OWN, LANES), F32)
    stage_back = pltpu.VMEM((3, peers * OWN, LANES), F32)
    send = pl.pallas_call(
        pack_kernel,
        out_shape=jax.ShapeDtypeStruct((peers, OWN, 5 * LANES), BF16),
        in_specs=[hbm] * 3,
        out_specs=vmem,
        scratch_shapes=[
            pltpu.VMEM((piece, channels), BF16),
            pltpu.VMEM((piece, channels), BF16),
            pltpu.VMEM(kernel_rows.shape, F32),
            stage_out,
            pltpu.SemaphoreType.DMA((3,)),
        ],
        compiler_params=fetching,
    )(inputs[0], grad_out[0], kernel_rows)
    recv = exchange(send)
    back = pl.pallas_call(
        correlate_kernel,
        out_shape=jax.ShapeDtypeStruct((peers, OWN, 3 * LANES), BF16),
        in_specs=[hbm, vmem],
        out_specs=vmem,
        scratch_shapes=[
            pltpu.SMEM(skip.shape, F32),
            pltpu.SemaphoreType.DMA(()),
            stage_out,
            pltpu.VMEM((OWN, 6, 2 * peers + 8, LANES), F32),
            pltpu.VMEM((OWN, 2, peers, LANES), F32),
            pltpu.VMEM((OWN, 16 * PIECES, LANES), F32),
            stage_back,
        ],
        compiler_params=params,
    )(skip, recv)
    landed = exchange(back)
    grad_inputs, grad_kernel = pl.pallas_call(
        unpack_kernel,
        out_shape=(
            jax.ShapeDtypeStruct((piece, channels), BF16),
            jax.ShapeDtypeStruct(kernel_rows.shape, F32),
        ),
        in_specs=[vmem],
        out_specs=(vmem, vmem),
        scratch_shapes=[stage_back],
        compiler_params=params,
    )(landed)
    return (grad_inputs[None], grad_kernel.T)


def solution(mesh):
    in_specs = (P("dp", "seq", "chan"), P("dp", "seq", "chan"), P("seq", ("chan", "dp")), P("chan"))
    out_specs = (P("dp", "seq", "chan"), P("seq", ("chan", "dp")))
    return jax.shard_map(shards, mesh=mesh, in_specs=in_specs, out_specs=out_specs, check_vma=False)
```

```python
import jax
import jax.numpy as jnp
from jax import lax
from jax.experimental import pallas as pl
from jax.experimental.pallas import tpu as pltpu
from jax.sharding import PartitionSpec as P

F32 = jnp.float32
BF16 = jnp.bfloat16
MESH_AXES = ("seq", "chan", "dp")
LANES = 128
OWN = 4
PIECES = 16
BATCH = 4
BLOCK = 64


def take(stage, first, count, stride, blocks):
    return jnp.concatenate([stage[b, pl.ds(first, count, stride=stride), :] for b in blocks], axis=1)


def put(stage, first, stride, values, blocks):
    for at, b in enumerate(blocks):
        part = values[:, at * LANES : (at + 1) * LANES]
        stage[b, pl.ds(first, values.shape[0], stride=stride), :] = part


def load_all(stage, ref):
    values = ref[...].astype(F32).reshape(stage.shape[1], -1)
    for b in range(stage.shape[0]):
        stage[b] = values[:, b * LANES : (b + 1) * LANES]


def store_all(ref, stage):
    values = jnp.concatenate([stage[b] for b in range(stage.shape[0])], axis=1)
    ref[...] = values.reshape(ref.shape).astype(BF16)


def pack_kernel(u_hbm, g_hbm, k_hbm, send_ref, u_ref, g_ref, k_ref, stage, sems):
    copies = [
        pltpu.make_async_copy(src, dst, sems.at[at])
        for at, (src, dst) in enumerate(((k_hbm, k_ref), (g_hbm, g_ref), (u_hbm, u_ref)))
    ]
    for copy in copies:
        copy.start()
    peers = send_ref.shape[0]
    copies[0].wait()
    k_rows = k_ref[...]
    high = k_rows.astype(BF16).astype(F32)
    low = k_rows - high
    for part, values in enumerate((high, low)):
        for half in range(2):
            put(stage, 2 * part + half, OWN, values[:, half * LANES : (half + 1) * LANES], (4,))
    for at, ref in ((1, g_ref), (2, u_ref)):
        copies[at].wait()
        rows = ref[...].astype(F32).T
        for e in range(OWN):
            put(stage, e, OWN, rows[e * peers : (e + 1) * peers], (2 * at - 2, 2 * at - 1))
    store_all(send_ref, stage)


def rows_of(b):
    return (1 - b // 2) * 2 * PIECES + (b % 2 + 1 - b // 2) % 2, 2


def correlate_kernel(skip_hbm, recv_ref, back_ref, skip_ref, sem, stage, blocks, result, partial_rows, out):
    peers = recv_ref.shape[0]
    fetch = pltpu.make_async_copy(skip_hbm, skip_ref, sem)
    fetch.start()
    first, step = rows_of(lax.axis_index("dp"))
    place = first + step * lax.axis_index("seq")
    piece = 2 * LANES
    load_all(stage, recv_ref)
    row_ids = lax.broadcasted_iota(jnp.int32, (LANES, LANES), 0)
    col_ids = lax.broadcasted_iota(jnp.int32, (LANES, LANES), 1)
    after = col_ids[0:BLOCK] > row_ids[0:BLOCK] + BLOCK
    flip_rows = lax.broadcasted_iota(jnp.int32, (piece, piece), 0)
    flip_cols = lax.broadcasted_iota(jnp.int32, (piece, piece), 1)
    flip = jnp.where(flip_cols == flip_rows + (BLOCK - 1) - 2 * (flip_rows % BLOCK), 1.0, 0.0).astype(BF16)
    turn = jnp.where((row_ids + col_ids) % LANES == 0, 1.0, 0.0).astype(BF16)
    stage[4] = jnp.dot(stage[4].astype(BF16), turn, preferred_element_type=F32)
    for e in range(OWN):
        for half in range(2):
            blocks[e, half, peers:, :] = jnp.zeros((peers + 8, LANES), F32)
            for kind in range(2):
                for b in range(BATCH):
                    first, step = rows_of(b)
                    values = stage[2 * kind + half, pl.ds(first * OWN + e, PIECES, stride=step * OWN), :]
                    blocks[e, 2 * kind + half, pl.ds(b, PIECES, stride=BATCH), :] = values
        k_first, k_step = rows_of(e)
        halves = [
            stage[4, pl.ds(k_first * OWN + half, PIECES, stride=k_step * OWN), :]
            + stage[4, pl.ds(k_first * OWN + 2 + half, PIECES, stride=k_step * OWN), :]
            for half in range(2)
        ]

        def later_blocks(half, lag):
            return blocks[e, half, BATCH * lag : BATCH * lag + peers, :].astype(BF16)

        def toeplitz_rows(block, before):
            values = halves[block % 2][block // 2 : block // 2 + 1, :]
            turned = pltpu.roll(jnp.broadcast_to(values, (LANES, LANES)), 0, 1, stride=1, stride_axis=0)
            square = jnp.where(col_ids <= row_ids, turned, before)
            high = square.astype(BF16)
            return jnp.concatenate([high, (square - high.astype(F32)).astype(BF16)], axis=1), turned

        def add_diagonals(block, turned, earlier):
            chosen = jnp.where(after, turned, earlier)
            partial_rows[e, 8 * block : 8 * block + 8, :] = jnp.sum(chosen.reshape(BLOCK // 8, 8, LANES), axis=0)

        left, right = blocks[e, 0, 0:peers, :], blocks[e, 1, 0:peers, :]
        following = blocks[e, 0, BATCH : peers + BATCH, :]
        blocks[e, 4, 0:peers, :] = jnp.concatenate([left[:, BLOCK:], right[:, :BLOCK]], axis=1)
        blocks[e, 5, 0:peers, :] = jnp.concatenate([right[:, BLOCK:], following[:, :BLOCK]], axis=1)
        for half in range(2):
            blocks[e, 4 + half, peers:, :] = jnp.zeros((peers + 8, LANES), F32)
        u_rows = jnp.concatenate([blocks[e, 2, 0:peers, :], blocks[e, 3, 0:peers, :]], axis=1).astype(BF16)
        u_turned = lax.dot_general(flip, u_rows, (((1,), (1,)), ((), ())), preferred_element_type=F32)
        u_turned = jnp.concatenate(
            [u_turned[at * BLOCK : (at + 1) * BLOCK] for at in (0, 2, 1, 3)], axis=1
        ).astype(BF16)
        before = jnp.zeros((LANES, LANES), F32)
        now = [later_blocks(at, 0) for at in (0, 4)]
        earlier = None
        both = None
        for step in range(PIECES):
            odd = [later_blocks(at, step) for at in (1, 5)]
            following = [later_blocks(at, step + 1) for at in (0, 4)]
            hankel = jnp.concatenate(
                [
                    jnp.concatenate(pair, axis=1)
                    for at in range(2)
                    for pair in ((now[at], odd[at]), (odd[at], following[at]))
                ],
                axis=0,
            )
            now = following
            first_rows, before = toeplitz_rows(2 * step, before)
            last_rows, before = toeplitz_rows(2 * step + 1, before)
            added = jnp.dot(
                hankel[0 : 2 * peers],
                jnp.concatenate([first_rows, last_rows], axis=0),
                preferred_element_type=F32,
            )
            both = added if both is None else both + added
            products = jnp.dot(u_turned, hankel, preferred_element_type=F32)
            for half in range(2):
                turned = pltpu.roll(
                    products[:, half * LANES : (half + 1) * LANES], BLOCK + 1, 1, stride=1, stride_axis=0
                )
                if earlier is not None:
                    add_diagonals(2 * step + half - 1, turned, earlier)
                earlier = turned
        add_diagonals(2 * PIECES - 1, jnp.zeros_like(earlier), earlier)
        for half in range(2):
            lags = sum(
                partial_rows[e, pl.ds(8 * half + row, PIECES, stride=16), :] for row in range(8)
            )
            high = lags.astype(BF16).astype(F32)
            for part, values in enumerate((high, lags - high)):
                first = k_first * OWN + 2 * part + half
                out[2, pl.ds(first, PIECES, stride=k_step * OWN), :] = values
        conv = both[:, 0:LANES] + both[:, LANES:]
        if e == 0:
            fetch.wait()
        gain = skip_ref[e * peers + place]
        for half in range(2):
            result[e, half] = conv[half * peers : (half + 1) * peers] + gain * blocks[e, half, 0:peers, :]
            for b in range(BATCH):
                first, step = rows_of(b)
                out[half, pl.ds(first * OWN + e, PIECES, stride=step * OWN), :] = result[
                    e, half, pl.ds(b, PIECES, stride=BATCH), :
                ]
    store_all(back_ref, out)


def unpack_kernel(recv_ref, grad_inputs_ref, grad_kernel_ref, stage):
    peers = recv_ref.shape[0]
    load_all(stage, recv_ref)
    rows = jnp.concatenate([take(stage, e, peers, OWN, (0, 1)) for e in range(OWN)], axis=0)
    grad_inputs_ref[...] = rows.T.astype(BF16)
    for half in range(2):
        grad_kernel_ref[:, half * LANES : (half + 1) * LANES] = take(
            stage, half, peers, OWN, (2,)
        ) + take(stage, 2 + half, peers, OWN, (2,))


def exchange(blocks):
    chans = lax.axis_size("chan")
    groups = []
    for chan in range(chans):
        group = [0] * (PIECES * BATCH)
        for b in range(BATCH):
            first, step = rows_of(b)
            for piece in range(PIECES):
                group[first + step * piece] = (piece * chans + chan) * BATCH + b
        groups.append(group)
    return lax.all_to_all(blocks, MESH_AXES, 0, 0, axis_index_groups=groups, tiled=True)


def shards(inputs, grad_out, kernel, skip):
    peers = PIECES * BATCH
    _, piece, channels = inputs.shape
    vmem = pl.BlockSpec(memory_space=pltpu.VMEM)
    hbm = pl.BlockSpec(memory_space=pltpu.HBM)
    params = pltpu.CompilerParams(vmem_limit_bytes=40 * 2**20)
    fetching = pltpu.CompilerParams(vmem_limit_bytes=60 * 2**20)
    kernel_rows = kernel.T
    stage_out = pltpu.VMEM((5, peers * OWN, LANES), F32)
    stage_back = pltpu.VMEM((3, peers * OWN, LANES), F32)
    send = pl.pallas_call(
        pack_kernel,
        out_shape=jax.ShapeDtypeStruct((peers, OWN, 5 * LANES), BF16),
        in_specs=[hbm] * 3,
        out_specs=vmem,
        scratch_shapes=[
            pltpu.VMEM((piece, channels), BF16),
            pltpu.VMEM((piece, channels), BF16),
            pltpu.VMEM(kernel_rows.shape, F32),
            stage_out,
            pltpu.SemaphoreType.DMA((3,)),
        ],
        compiler_params=fetching,
    )(inputs[0], grad_out[0], kernel_rows)
    recv = exchange(send)
    back = pl.pallas_call(
        correlate_kernel,
        out_shape=jax.ShapeDtypeStruct((peers, OWN, 3 * LANES), BF16),
        in_specs=[hbm, vmem],
        out_specs=vmem,
        scratch_shapes=[
            pltpu.SMEM(skip.shape, F32),
            pltpu.SemaphoreType.DMA(()),
            stage_out,
            pltpu.VMEM((OWN, 6, 2 * peers + 8, LANES), F32),
            pltpu.VMEM((OWN, 2, peers, LANES), F32),
            pltpu.VMEM((OWN, 16 * PIECES, LANES), F32),
            stage_back,
        ],
        compiler_params=params,
    )(skip, recv)
    landed = exchange(back)
    grad_inputs, grad_kernel = pl.pallas_call(
        unpack_kernel,
        out_shape=(
            jax.ShapeDtypeStruct((piece, channels), BF16),
            jax.ShapeDtypeStruct(kernel_rows.shape, F32),
        ),
        in_specs=[vmem],
        out_specs=(vmem, vmem),
        scratch_shapes=[stage_back],
        compiler_params=params,
    )(landed)
    return (grad_inputs[None], grad_kernel.T)


def solution(mesh):
    in_specs = (P("dp", "seq", "chan"), P("dp", "seq", "chan"), P("seq", ("chan", "dp")), P("chan"))
    out_specs = (P("dp", "seq", "chan"), P("seq", ("chan", "dp")))
    return jax.shard_map(shards, mesh=mesh, in_specs=in_specs, out_specs=out_specs, check_vma=False)
```

```python
import jax
import jax.numpy as jnp
from jax import lax
from jax.experimental import pallas as pl
from jax.experimental.pallas import tpu as pltpu
from jax.sharding import PartitionSpec as P

F32 = jnp.float32
BF16 = jnp.bfloat16
MESH_AXES = ("seq", "chan", "dp")
LANES = 128
OWN = 4
PIECES = 16
BATCH = 4
BLOCK = 64


def take(stage, first, count, stride, blocks):
    return jnp.concatenate([stage[b, pl.ds(first, count, stride=stride), :] for b in blocks], axis=1)


def put(stage, first, stride, values, blocks):
    for at, b in enumerate(blocks):
        part = values[:, at * LANES : (at + 1) * LANES]
        stage[b, pl.ds(first, values.shape[0], stride=stride), :] = part


def load_all(stage, ref):
    values = ref[...].astype(F32).reshape(stage.shape[1], -1)
    for b in range(stage.shape[0]):
        stage[b] = values[:, b * LANES : (b + 1) * LANES]


def store_all(ref, stage):
    values = jnp.concatenate([stage[b] for b in range(stage.shape[0])], axis=1)
    ref[...] = values.reshape(ref.shape).astype(BF16)


def pack_kernel(u_hbm, g_hbm, k_hbm, send_ref, u_ref, g_ref, k_ref, stage, sems):
    copies = [
        pltpu.make_async_copy(src, dst, sems.at[at])
        for at, (src, dst) in enumerate(((k_hbm, k_ref), (g_hbm, g_ref), (u_hbm, u_ref)))
    ]
    for copy in copies:
        copy.start()
    peers = send_ref.shape[0]
    copies[0].wait()
    k_rows = k_ref[...]
    high = k_rows.astype(BF16).astype(F32)
    low = k_rows - high
    for part, values in enumerate((high, low)):
        for half in range(2):
            put(stage, 2 * part + half, OWN, values[:, half * LANES : (half + 1) * LANES], (4,))
    for at, ref in ((1, g_ref), (2, u_ref)):
        copies[at].wait()
        rows = ref[...].astype(F32).T
        for e in range(OWN):
            put(stage, e, OWN, rows[e * peers : (e + 1) * peers], (2 * at - 2, 2 * at - 1))
    store_all(send_ref, stage)


def rows_of(b):
    return (b + 2) % BATCH, BATCH


def correlate_kernel(skip_hbm, recv_ref, back_ref, skip_ref, sem, stage, blocks, result, partial_rows, out):
    peers = recv_ref.shape[0]
    fetch = pltpu.make_async_copy(skip_hbm, skip_ref, sem)
    fetch.start()
    first, step = rows_of(lax.axis_index("dp"))
    place = first + step * lax.axis_index("seq")
    piece = 2 * LANES
    load_all(stage, recv_ref)
    row_ids = lax.broadcasted_iota(jnp.int32, (LANES, LANES), 0)
    col_ids = lax.broadcasted_iota(jnp.int32, (LANES, LANES), 1)
    after = col_ids[0:BLOCK] > row_ids[0:BLOCK] + BLOCK
    flip_rows = lax.broadcasted_iota(jnp.int32, (piece, piece), 0)
    flip_cols = lax.broadcasted_iota(jnp.int32, (piece, piece), 1)
    flip = jnp.where(flip_cols == flip_rows + (BLOCK - 1) - 2 * (flip_rows % BLOCK), 1.0, 0.0).astype(BF16)
    turn = jnp.where((row_ids + col_ids) % LANES == 0, 1.0, 0.0).astype(BF16)
    stage[4] = jnp.dot(stage[4].astype(BF16), turn, preferred_element_type=F32)
    for e in range(OWN):
        for half in range(2):
            blocks[e, half, peers:, :] = jnp.zeros((peers + 8, LANES), F32)
            for kind in range(2):
                for b in range(BATCH):
                    first, step = rows_of(b)
                    values = stage[2 * kind + half, pl.ds(first * OWN + e, PIECES, stride=step * OWN), :]
                    blocks[e, 2 * kind + half, pl.ds(b, PIECES, stride=BATCH), :] = values
        k_first, k_step = rows_of(e)
        halves = [
            stage[4, pl.ds(k_first * OWN + half, PIECES, stride=k_step * OWN), :]
            + stage[4, pl.ds(k_first * OWN + 2 + half, PIECES, stride=k_step * OWN), :]
            for half in range(2)
        ]

        def later_blocks(half, lag):
            return blocks[e, half, BATCH * lag : BATCH * lag + peers, :].astype(BF16)

        def toeplitz_rows(block, before):
            values = halves[block % 2][block // 2 : block // 2 + 1, :]
            turned = pltpu.roll(jnp.broadcast_to(values, (LANES, LANES)), 0, 1, stride=1, stride_axis=0)
            square = jnp.where(col_ids <= row_ids, turned, before)
            high = square.astype(BF16)
            return jnp.concatenate([high, (square - high.astype(F32)).astype(BF16)], axis=1), turned

        def add_diagonals(block, turned, earlier):
            chosen = jnp.where(after, turned, earlier)
            partial_rows[e, 8 * block : 8 * block + 8, :] = jnp.sum(chosen.reshape(BLOCK // 8, 8, LANES), axis=0)

        left, right = blocks[e, 0, 0:peers, :], blocks[e, 1, 0:peers, :]
        following = blocks[e, 0, BATCH : peers + BATCH, :]
        blocks[e, 4, 0:peers, :] = jnp.concatenate([left[:, BLOCK:], right[:, :BLOCK]], axis=1)
        blocks[e, 5, 0:peers, :] = jnp.concatenate([right[:, BLOCK:], following[:, :BLOCK]], axis=1)
        for half in range(2):
            blocks[e, 4 + half, peers:, :] = jnp.zeros((peers + 8, LANES), F32)
        u_rows = jnp.concatenate([blocks[e, 2, 0:peers, :], blocks[e, 3, 0:peers, :]], axis=1).astype(BF16)
        u_turned = lax.dot_general(flip, u_rows, (((1,), (1,)), ((), ())), preferred_element_type=F32)
        u_turned = jnp.concatenate(
            [u_turned[at * BLOCK : (at + 1) * BLOCK] for at in (0, 2, 1, 3)], axis=1
        ).astype(BF16)
        before = jnp.zeros((LANES, LANES), F32)
        now = [later_blocks(at, 0) for at in (0, 4)]
        earlier = None
        both = None
        for step in range(PIECES):
            odd = [later_blocks(at, step) for at in (1, 5)]
            following = [later_blocks(at, step + 1) for at in (0, 4)]
            hankel = jnp.concatenate(
                [
                    jnp.concatenate(pair, axis=1)
                    for at in range(2)
                    for pair in ((now[at], odd[at]), (odd[at], following[at]))
                ],
                axis=0,
            )
            now = following
            first_rows, before = toeplitz_rows(2 * step, before)
            last_rows, before = toeplitz_rows(2 * step + 1, before)
            added = jnp.dot(
                hankel[0 : 2 * peers],
                jnp.concatenate([first_rows, last_rows], axis=0),
                preferred_element_type=F32,
            )
            both = added if both is None else both + added
            products = jnp.dot(u_turned, hankel, preferred_element_type=F32)
            for half in range(2):
                turned = pltpu.roll(
                    products[:, half * LANES : (half + 1) * LANES], BLOCK + 1, 1, stride=1, stride_axis=0
                )
                if earlier is not None:
                    add_diagonals(2 * step + half - 1, turned, earlier)
                earlier = turned
        add_diagonals(2 * PIECES - 1, jnp.zeros_like(earlier), earlier)
        for half in range(2):
            lags = sum(
                partial_rows[e, pl.ds(8 * half + row, PIECES, stride=16), :] for row in range(8)
            )
            high = lags.astype(BF16).astype(F32)
            for part, values in enumerate((high, lags - high)):
                first = k_first * OWN + 2 * part + half
                out[2, pl.ds(first, PIECES, stride=k_step * OWN), :] = values
        conv = both[:, 0:LANES] + both[:, LANES:]
        if e == 0:
            fetch.wait()
        gain = skip_ref[e * peers + place]
        for half in range(2):
            result[e, half] = conv[half * peers : (half + 1) * peers] + gain * blocks[e, half, 0:peers, :]
            for b in range(BATCH):
                first, step = rows_of(b)
                out[half, pl.ds(first * OWN + e, PIECES, stride=step * OWN), :] = result[
                    e, half, pl.ds(b, PIECES, stride=BATCH), :
                ]
    store_all(back_ref, out)


def unpack_kernel(recv_ref, grad_inputs_ref, grad_kernel_ref, stage):
    peers = recv_ref.shape[0]
    load_all(stage, recv_ref)
    rows = jnp.concatenate([take(stage, e, peers, OWN, (0, 1)) for e in range(OWN)], axis=0)
    grad_inputs_ref[...] = rows.T.astype(BF16)
    for half in range(2):
        grad_kernel_ref[:, half * LANES : (half + 1) * LANES] = take(
            stage, half, peers, OWN, (2,)
        ) + take(stage, 2 + half, peers, OWN, (2,))


def exchange(blocks):
    chans = lax.axis_size("chan")
    groups = []
    for chan in range(chans):
        group = [0] * (PIECES * BATCH)
        for b in range(BATCH):
            first, step = rows_of(b)
            for piece in range(PIECES):
                group[first + step * piece] = (piece * chans + chan) * BATCH + b
        groups.append(group)
    return lax.all_to_all(blocks, MESH_AXES, 0, 0, axis_index_groups=groups, tiled=True)


def shards(inputs, grad_out, kernel, skip):
    peers = PIECES * BATCH
    _, piece, channels = inputs.shape
    vmem = pl.BlockSpec(memory_space=pltpu.VMEM)
    hbm = pl.BlockSpec(memory_space=pltpu.HBM)
    params = pltpu.CompilerParams(vmem_limit_bytes=40 * 2**20)
    fetching = pltpu.CompilerParams(vmem_limit_bytes=60 * 2**20)
    kernel_rows = kernel.T
    stage_out = pltpu.VMEM((5, peers * OWN, LANES), F32)
    stage_back = pltpu.VMEM((3, peers * OWN, LANES), F32)
    send = pl.pallas_call(
        pack_kernel,
        out_shape=jax.ShapeDtypeStruct((peers, OWN, 5 * LANES), BF16),
        in_specs=[hbm] * 3,
        out_specs=vmem,
        scratch_shapes=[
            pltpu.VMEM((piece, channels), BF16),
            pltpu.VMEM((piece, channels), BF16),
            pltpu.VMEM(kernel_rows.shape, F32),
            stage_out,
            pltpu.SemaphoreType.DMA((3,)),
        ],
        compiler_params=fetching,
    )(inputs[0], grad_out[0], kernel_rows)
    recv = exchange(send)
    back = pl.pallas_call(
        correlate_kernel,
        out_shape=jax.ShapeDtypeStruct((peers, OWN, 3 * LANES), BF16),
        in_specs=[hbm, vmem],
        out_specs=vmem,
        scratch_shapes=[
            pltpu.SMEM(skip.shape, F32),
            pltpu.SemaphoreType.DMA(()),
            stage_out,
            pltpu.VMEM((OWN, 6, 2 * peers + 8, LANES), F32),
            pltpu.VMEM((OWN, 2, peers, LANES), F32),
            pltpu.VMEM((OWN, 16 * PIECES, LANES), F32),
            stage_back,
        ],
        compiler_params=params,
    )(skip, recv)
    landed = exchange(back)
    grad_inputs, grad_kernel = pl.pallas_call(
        unpack_kernel,
        out_shape=(
            jax.ShapeDtypeStruct((piece, channels), BF16),
            jax.ShapeDtypeStruct(kernel_rows.shape, F32),
        ),
        in_specs=[vmem],
        out_specs=(vmem, vmem),
        scratch_shapes=[stage_back],
        compiler_params=params,
    )(landed)
    return (grad_inputs[None], grad_kernel.T)


def solution(mesh):
    in_specs = (P("dp", "seq", "chan"), P("dp", "seq", "chan"), P("seq", ("chan", "dp")), P("chan"))
    out_specs = (P("dp", "seq", "chan"), P("seq", ("chan", "dp")))
    return jax.shard_map(shards, mesh=mesh, in_specs=in_specs, out_specs=out_specs, check_vma=False)
```
